256 devices in a mesh: req: 128 (over y_hi, x, z, core), head: 2 (over y_lo).
Axes of the slice: x: 4, y: 4 (y_hi: 2, y_lo: 2; y = y_hi * 2 + y_lo), z: 8, core: 2. Of those that a mesh axis runs over, the one named last changes fastest.
Arguments:
- queries: bfloat16 [128, 256, 8192], P('req', None, 'head'), may hold values from -17 to 17
- suffix_keys: bfloat16 [128, 256, 1024], P('req', None, 'head'), may hold values from -6 to 6
- suffix_values: bfloat16 [128, 256, 1024], P('req', None, 'head'), may hold values from -6 to 6
- node_keys: bfloat16 [256, 256, 1024], P(('req', 'head')), may hold values from -6 to 6
- node_values: bfloat16 [256, 256, 1024], P(('req', 'head')), may hold values from -6 to 6
- parents: int32 [256], P(('req', 'head')), may hold values from -1 to 255, as said below
- node_len: int32 [256], P(('req', 'head')), may hold values from 1 to 256
- req_leaf: int32 [128], P('req'), may hold values from 0 to 255, as said below
Outputs:
- attended: bfloat16 [128, 256, 8192], P('req', None, 'head')
The draws below stay inside these ranges and needn't reach their ends.
Inputs may be any that keep to these rules, and one draw needn't show every extreme that they name: Following parents from any node reaches a root (-1) within 4 steps. `req_leaf`: each request's leaf lies exactly 3 parent steps below a root.
All inputs are finite; a program needn't handle non-finite values.
Results may differ from the reference program's by a relative error of at most 0.006.
Values may be sent and summed in bfloat16 or wider, within the bound.
No kernel may reach another device: no remote copies, remote signals or barrier semaphores. Data moves between devices by JAX's collectives and lax.ppermute only.
A program may use at most 64 MiB of HBM per device.

```python
import jax
import jax.numpy as jnp
from jax import lax

HEADS = 64
KV_HEADS = 8
HEAD_DIM = 128
SUF = 256
NODE_TOK = 256
DEPTH = 4
GROUP = 8
REQS = 128
NODES = 256


def tree_ordering(key):
    middle_end = NODES // 4
    base = 1 + jax.random.permutation(jax.random.fold_in(key, 101), NODES - 3)
    return jnp.concatenate([base[:middle_end], jnp.array([NODES - 2], jnp.int32), base[middle_end:].astype(jnp.int32), jnp.array([0, NODES - 1], jnp.int32)]).astype(jnp.int32)


def draw_queries(key, part):
    key = jax.random.fold_in(key, 3)
    drawn = jnp.clip(jax.random.normal(key, (REQS, SUF, HEADS * HEAD_DIM), jnp.float32), -6.0, 6.0)
    return drawn.astype(jnp.bfloat16)


def draw_suffix_keys(key, part):
    key = jax.random.fold_in(key, 5)
    drawn = jnp.clip(jax.random.normal(key, (REQS, SUF, KV_HEADS * HEAD_DIM), jnp.float32), -6.0, 6.0)
    return drawn.astype(jnp.bfloat16)


def draw_parents(key, part):
    ordering = tree_ordering(key)
    key = jax.random.fold_in(key, 7)
    roots_end = NODES // 16
    middle_end = NODES // 4
    upper_end = NODES // 2
    ranking = jnp.argsort(ordering).astype(jnp.int32)
    lowest = jnp.where(ranking < middle_end, 0, jnp.where(ranking < upper_end, roots_end, middle_end))
    highest = jnp.where(ranking < middle_end, roots_end, jnp.where(ranking < upper_end, middle_end, upper_end))
    samples = jax.random.randint(key, (NODES,), 0, 1 << 20)
    chosen_rank = lowest + samples % (highest - lowest)
    chosen_rank = jnp.where(ranking == NODES - 1, middle_end, chosen_rank)
    return jnp.where(ranking < roots_end, -1, ordering[chosen_rank]).astype(jnp.int32)


def draw_req_leaf(key, part):
    ordering = tree_ordering(key)
    key = jax.random.fold_in(key, 9)
    samples = jax.random.randint(key, (REQS,), NODES // 2, NODES)
    samples = samples.at[0].set(NODES - 2).at[1].set(NODES - 1)
    return ordering[samples].astype(jnp.int32)


def place_ends(values, stream_key, low, top_value):
    longest = values.shape.index(max(values.shape))
    spots = []
    for shift in (0, 1):
        where = [jax.random.randint(jax.random.fold_in(stream_key, axis), (), 0, length) for axis, length in enumerate(values.shape)]
        where[longest] = (where[longest] + shift) % values.shape[longest]
        spots.append(tuple(where))
    return values.at[spots[0]].set(low).at[spots[1]].set(top_value)


def block_levels(stream_key, extent, cuts, least, high):
    gain, own = 1.0, jax.random.fold_in(stream_key, 6)
    for position, parts in cuts:
        heights = jnp.exp(jax.random.uniform(jax.random.fold_in(own, position), (parts,), jnp.float32, least / len(cuts), high / len(cuts)))
        gain = gain * jnp.repeat(heights, extent[position] // parts).reshape([-1 if axis == position else 1 for axis in range(len(extent))])
    return gain


def bell_draw(rng, dims, width, limit, shards=(), held_as=jnp.bfloat16):
    factor_of = block_levels(rng, dims, shards, -0.22, 0.18) if shards else 1.0
    entries = jax.random.normal(rng, dims, jnp.float32) * width * factor_of
    return jnp.minimum(jnp.maximum(entries, -limit), limit).astype(held_as)


def setup_inputs(seed: int = 0) -> dict:
    keys = jax.random.split(jax.random.key(seed), 9)
    return {
        "queries": draw_queries(jax.random.fold_in(keys[8], 71), 0),
        "suffix_keys": draw_suffix_keys(jax.random.fold_in(keys[8], 71), 0),
        "suffix_values": bell_draw(keys[2], (REQS, SUF, KV_HEADS * HEAD_DIM), 1.0, 6.0, ((0, 128), (2, 2))),
        "node_keys": bell_draw(keys[3], (NODES, NODE_TOK, KV_HEADS * HEAD_DIM), 1.0, 6.0, ((0, 256),)),
        "node_values": bell_draw(keys[4], (NODES, NODE_TOK, KV_HEADS * HEAD_DIM), 1.0, 6.0, ((0, 256),)),
        "parents": draw_parents(jax.random.fold_in(keys[8], 71), 0),
        "node_len": place_ends(jax.random.randint(keys[6], (NODES,), 1, NODE_TOK + 1), jax.random.fold_in(keys[6], 1), 1, NODE_TOK).astype(jnp.int32),
        "req_leaf": draw_req_leaf(jax.random.fold_in(keys[8], 71), 0),
    }


def reference(queries, suffix_keys, suffix_values, node_keys, node_values, parents, node_len, req_leaf):
    positions = jnp.arange(SUF, dtype=jnp.int32)
    causal = positions[:, None] >= positions[None, :]
    slot_ids = jnp.arange(NODE_TOK, dtype=jnp.int32)

    def attend_request(request):
        lineage = [req_leaf[request]]
        for depth_step in range(DEPTH - 1):
            lineage.append(parents[lineage[-1]])
        ancestry = jnp.stack(lineage).astype(jnp.int32)
        prefix_keys = node_keys[ancestry].reshape(DEPTH * NODE_TOK, KV_HEADS, HEAD_DIM)
        prefix_values = node_values[ancestry].reshape(DEPTH * NODE_TOK, KV_HEADS, HEAD_DIM)
        present = (slot_ids[None, :] < node_len[ancestry][:, None]).reshape(-1)
        own_keys = suffix_keys[request].reshape(SUF, KV_HEADS, HEAD_DIM)
        own_values = suffix_values[request].reshape(SUF, KV_HEADS, HEAD_DIM)
        all_keys = jnp.concatenate([prefix_keys, own_keys], axis=0).astype(jnp.float32)
        all_values = jnp.concatenate([prefix_values, own_values], axis=0).astype(jnp.float32)
        visible = jnp.concatenate([jnp.broadcast_to(present[None, :], (SUF, DEPTH * NODE_TOK)), causal], axis=1)
        query_rows = queries[request].reshape(SUF, KV_HEADS, GROUP, HEAD_DIM).astype(jnp.float32)
        scores = jnp.einsum("tkgd,skd->tkgs", query_rows, all_keys) * (HEAD_DIM ** -0.5)
        scores = jnp.where(visible[:, None, None, :], scores, -jnp.inf)
        row_max = jnp.max(scores, axis=-1, keepdims=True)
        weights = jnp.where(visible[:, None, None, :], jnp.exp(scores - row_max), 0.0)
        totals = jnp.sum(weights, axis=-1)
        rounded = lax.optimization_barrier(weights.astype(jnp.bfloat16)).astype(jnp.float32)
        output = jnp.einsum("tkgs,skd->tkgd", rounded, all_values) / totals[..., None]
        return output.reshape(SUF, HEADS * HEAD_DIM).astype(jnp.bfloat16)

    return lax.map(attend_request, jnp.arange(REQS, dtype=jnp.int32))
```

```python
import functools
import math

import jax
import jax.numpy as jnp
from jax import lax
from jax.experimental import pallas as pl
from jax.experimental.pallas import tpu as pltpu
from jax.sharding import PartitionSpec as P

HEAD_DIM = 128
DEPTH = 4
BLK = 16
LOW = -1e30


def spread_kernel(keys_ref, values_ref, out_ref):
    tok_blocks = keys_ref.shape[0] // BLK
    heads_all = keys_ref.shape[1] // HEAD_DIM
    heads = heads_all // 2
    for kv, ref in enumerate((keys_ref, values_ref)):
        for b in range(tok_blocks):
            for col in range(heads_all):
                group, j = divmod(col, heads)
                piece = (kv * heads + j) * tok_blocks + b
                out_ref[piece * 2 + group] = ref[
                    b * BLK:(b + 1) * BLK, col * HEAD_DIM:(col + 1) * HEAD_DIM
                ]


def spread(keys, values):
    tok, width = keys.shape
    pieces = 2 * (tok // BLK) * (width // HEAD_DIM)
    return pl.pallas_call(
        spread_kernel,
        out_shape=jax.ShapeDtypeStruct((pieces, BLK, HEAD_DIM), keys.dtype),
        in_specs=[pl.BlockSpec(memory_space=pltpu.VMEM)] * 2,
        out_specs=pl.BlockSpec(memory_space=pltpu.VMEM),
        compiler_params=pltpu.CompilerParams(vmem_limit_bytes=32 << 20),
    )(keys, values)


def pick_kernel(reqs_step, table_ref, pieces_ref, out_ref):
    nodes = pieces_ref.shape[0]
    base = pl.program_id(0) * reqs_step

    def one(r, carry):
        node = table_ref[2 * nodes + 2 * (base + r)]
        for i in range(DEPTH):
            out_ref[r, i * BLK:(i + 1) * BLK, :] = pieces_ref[node]
            if i < DEPTH - 1:
                node = table_ref[node]
        return carry

    lax.fori_loop(0, reqs_step, one, 0, unroll=8)


def pick(table, pieces, reqs):
    steps = 4
    reqs_step = reqs // steps
    return pl.pallas_call(
        functools.partial(pick_kernel, reqs_step),
        out_shape=jax.ShapeDtypeStruct((reqs, DEPTH * BLK, HEAD_DIM), pieces.dtype),
        grid_spec=pltpu.PrefetchScalarGridSpec(
            num_scalar_prefetch=1,
            grid=(steps,),
            in_specs=[pl.BlockSpec(pieces.shape, lambda s, t: (0, 0, 0))],
            out_specs=pl.BlockSpec((reqs_step, DEPTH * BLK, HEAD_DIM), lambda s, t: (s, 0, 0)),
        ),
        compiler_params=pltpu.CompilerParams(vmem_limit_bytes=32 << 20),
    )(table, pieces)


def attend_kernel(
    table_ref, me_ref, query_ref, sk_ref, sv_ref, pk_ref, pv_ref, out_ref,
    key_scr, val_scr, sval_scr,
):
    nodes = table_ref.shape[0] // 4
    blocks = pk_ref.shape[0]
    rows = DEPTH * BLK
    suf = sk_ref.shape[0]
    factor = math.log2(math.e) / math.sqrt(HEAD_DIM)

    node = table_ref[2 * nodes + 2 * me_ref[0]]
    spans = []
    for i in range(DEPTH):
        spans.append(table_ref[nodes + node])
        if i < DEPTH - 1:
            node = table_ref[node]
    tok = lax.broadcasted_iota(jnp.int32, (blocks, BLK, HEAD_DIM), 0) * BLK
    tok = tok + lax.broadcasted_iota(jnp.int32, (blocks, BLK, HEAD_DIM), 1)
    for i in range(DEPTH):
        here = slice(i * BLK, (i + 1) * BLK)
        seen = tok < spans[i]
        first = pk_ref[0, i * BLK:i * BLK + 1, :].astype(jnp.float32)
        keys = jnp.where(seen, pk_ref[:, here, :].astype(jnp.float32), first[None])
        values = jnp.where(seen, pv_ref[:, here, :].astype(jnp.float32), 0.0)
        key_scr[:, here, :] = keys.astype(jnp.bfloat16)
        val_scr[:, here, :HEAD_DIM] = values.astype(jnp.bfloat16)
        val_scr[:, here, HEAD_DIM:] = seen.astype(jnp.float32).astype(jnp.bfloat16)
    sval_scr[:, :HEAD_DIM] = sv_ref[...]
    sval_scr[:, HEAD_DIM:] = jnp.ones((suf, HEAD_DIM), jnp.bfloat16)

    pkeys = key_scr[...].reshape(blocks * rows, HEAD_DIM)
    pvals = val_scr[...].reshape(blocks * rows, 2 * HEAD_DIM)
    skeys = sk_ref[...]
    svals = sval_scr[...]
    causal = lax.broadcasted_iota(jnp.int32, (suf, suf), 0) >= lax.broadcasted_iota(
        jnp.int32, (suf, suf), 1
    )
    over = (((1,), (1,)), ((), ()))
    for g in range(query_ref.shape[1] // HEAD_DIM):
        cols = slice(g * HEAD_DIM, (g + 1) * HEAD_DIM)
        query = query_ref[:, cols]
        s1 = lax.dot_general(query, pkeys, over, preferred_element_type=jnp.float32)
        s2 = lax.dot_general(query, skeys, over, preferred_element_type=jnp.float32)
        s2 = jnp.where(causal, s2, LOW)
        top = jnp.maximum(
            jnp.max(s1, axis=1, keepdims=True), jnp.max(s2, axis=1, keepdims=True)
        )
        w1 = jnp.exp2((s1 - top) * factor).astype(jnp.bfloat16)
        w2 = jnp.exp2((s2 - top) * factor).astype(jnp.bfloat16)
        sums = jnp.dot(w1, pvals, preferred_element_type=jnp.float32)
        sums = sums + jnp.dot(w2, svals, preferred_element_type=jnp.float32)
        out_ref[:, cols] = (sums[:, :HEAD_DIM] / sums[:, HEAD_DIM:]).astype(out_ref.dtype)


def attend(table, me, queries, suffix_keys, suffix_values, prefix):
    suf, width = queries.shape
    heads = suffix_keys.shape[1] // HEAD_DIM
    blocks = prefix.shape[0] // (2 * heads)
    qwidth = width // heads
    rows = DEPTH * BLK
    return pl.pallas_call(
        attend_kernel,
        out_shape=jax.ShapeDtypeStruct((suf, width), jnp.bfloat16),
        grid_spec=pltpu.PrefetchScalarGridSpec(
            num_scalar_prefetch=2,
            grid=(heads,),
            in_specs=[
                pl.BlockSpec((suf, qwidth), lambda j, *_: (0, j)),
                pl.BlockSpec((suf, HEAD_DIM), lambda j, *_: (0, j)),
                pl.BlockSpec((suf, HEAD_DIM), lambda j, *_: (0, j)),
                pl.BlockSpec((blocks, rows, HEAD_DIM), lambda j, *_: (j, 0, 0)),
                pl.BlockSpec((blocks, rows, HEAD_DIM), lambda j, *_: (heads + j, 0, 0)),
            ],
            out_specs=pl.BlockSpec((suf, qwidth), lambda j, *_: (0, j)),
            scratch_shapes=[
                pltpu.VMEM((blocks, rows, HEAD_DIM), jnp.bfloat16),
                pltpu.VMEM((blocks, rows, 2 * HEAD_DIM), jnp.bfloat16),
                pltpu.VMEM((suf, 2 * HEAD_DIM), jnp.bfloat16),
            ],
        ),
        compiler_params=pltpu.CompilerParams(vmem_limit_bytes=48 << 20),
    )(table, me, queries, suffix_keys, suffix_values, prefix, prefix)


def share_ints(parents, node_len, req_leaf):
    axes = ("req", "head")
    count = lax.axis_size("req") * lax.axis_size("head")
    me = lax.axis_index("req") * lax.axis_size("head") + lax.axis_index("head")
    slots = jnp.arange(count, dtype=jnp.int32) == me
    zero = jnp.zeros((count,), jnp.int32)
    table = jnp.concatenate(
        [jnp.where(slots, x[0], 0) for x in (parents, node_len, req_leaf)] + [zero]
    )
    table = table.reshape(-1, 128)
    bit = 1
    while bit < count:
        table = table + lax.ppermute(table, axes, [(i, i ^ bit) for i in range(count)])
        bit *= 2
    return table.reshape(-1)


def per_device(
    queries, suffix_keys, suffix_values, node_keys, node_values, parents, node_len, req_leaf
):
    reqs = lax.axis_size("req")
    sent = spread(node_keys[0], node_values[0])
    pieces = lax.all_to_all(sent, ("req", "head"), split_axis=0, concat_axis=0, tiled=True)
    table = share_ints(parents, node_len, req_leaf)
    picked = pick(table, pieces, reqs)
    prefix = lax.all_to_all(picked, "req", split_axis=0, concat_axis=0, tiled=True)
    me = lax.axis_index("req").reshape(1)
    out = attend(table, me, queries[0], suffix_keys[0], suffix_values[0], prefix)
    return out[None]


def solution(mesh):
    in_specs = (
        P("req", None, "head"),
        P("req", None, "head"),
        P("req", None, "head"),
        P(("req", "head"), None, None),
        P(("req", "head"), None, None),
        P(("req", "head")),
        P(("req", "head")),
        P("req"),
    )
    out_specs = P("req", None, "head")
    return jax.shard_map(
        per_device, mesh=mesh, in_specs=in_specs, out_specs=out_specs, check_vma=False
    )
```

```python
import functools
import math

import jax
import jax.numpy as jnp
from jax import lax
from jax.experimental import pallas as pl
from jax.experimental.pallas import tpu as pltpu
from jax.sharding import PartitionSpec as P

HEAD_DIM = 128
DEPTH = 4
BLK = 16
LOW = -1e30


def spread_kernel(keys_ref, values_ref, out_ref, sems):
    _, heads, _, groups, _, _ = out_ref.shape
    copies = []
    for kv, ref in enumerate((keys_ref, values_ref)):
        for group in range(groups):
            for j in range(heads):
                col = (group * heads + j) * HEAD_DIM
                copies.append(
                    pltpu.make_async_copy(
                        ref.at[:, :, col:col + HEAD_DIM],
                        out_ref.at[kv, j, :, group],
                        sems.at[len(copies)],
                    )
                )
    for copy in copies:
        copy.start()
    for copy in copies:
        copy.wait()


def spread(keys, values, groups):
    tok, width = keys.shape
    blocks, heads = tok // BLK, width // HEAD_DIM // groups
    out = pl.pallas_call(
        spread_kernel,
        out_shape=jax.ShapeDtypeStruct((2, heads, blocks, groups, BLK, HEAD_DIM), keys.dtype),
        in_specs=[pl.BlockSpec(memory_space=pl.ANY)] * 2,
        out_specs=pl.BlockSpec(memory_space=pl.ANY),
        scratch_shapes=[pltpu.SemaphoreType.DMA((2 * groups * heads,))],
        compiler_params=pltpu.CompilerParams(vmem_limit_bytes=60 << 20),
    )(keys.reshape(blocks, BLK, width), values.reshape(blocks, BLK, width))
    return out.reshape(-1, BLK, HEAD_DIM)


def pick_kernel(reqs_step, table_ref, pieces_ref, out_ref):
    nodes = pieces_ref.shape[0]
    base = pl.program_id(0) * reqs_step

    def one(r, carry):
        node = table_ref[2 * nodes + 2 * (base + r)]
        for i in range(DEPTH):
            out_ref[r, i * BLK:(i + 1) * BLK, :] = pieces_ref[node]
            if i < DEPTH - 1:
                node = table_ref[node]
        return carry

    lax.fori_loop(0, reqs_step, one, 0, unroll=8)


def pick(table, pieces, reqs):
    steps = 4
    reqs_step = reqs // steps
    return pl.pallas_call(
        functools.partial(pick_kernel, reqs_step),
        out_shape=jax.ShapeDtypeStruct((reqs, DEPTH * BLK, HEAD_DIM), pieces.dtype),
        grid_spec=pltpu.PrefetchScalarGridSpec(
            num_scalar_prefetch=1,
            grid=(steps,),
            in_specs=[pl.BlockSpec(pieces.shape, lambda s, t: (0, 0, 0))],
            out_specs=pl.BlockSpec((reqs_step, DEPTH * BLK, HEAD_DIM), lambda s, t: (s, 0, 0)),
        ),
        compiler_params=pltpu.CompilerParams(vmem_limit_bytes=32 << 20),
    )(table, pieces)


def attend_kernel(
    table_ref, me_ref, query_ref, sk_ref, sv_ref, pk_ref, pv_ref, out_ref,
    key_scr, val_scr, sval_scr,
):
    nodes = table_ref.shape[0] // 4
    blocks = pk_ref.shape[0]
    rows = DEPTH * BLK
    suf = sk_ref.shape[0]
    factor = math.log2(math.e) / math.sqrt(HEAD_DIM)

    node = table_ref[2 * nodes + 2 * me_ref[0]]
    spans = []
    for i in range(DEPTH):
        spans.append(table_ref[nodes + node])
        if i < DEPTH - 1:
            node = table_ref[node]
    tok = lax.broadcasted_iota(jnp.int32, (blocks, BLK, HEAD_DIM), 0) * BLK
    tok = tok + lax.broadcasted_iota(jnp.int32, (blocks, BLK, HEAD_DIM), 1)
    for i in range(DEPTH):
        here = slice(i * BLK, (i + 1) * BLK)
        seen = tok < spans[i]
        first = pk_ref[0, i * BLK:i * BLK + 1, :].astype(jnp.float32)
        keys = jnp.where(seen, pk_ref[:, here, :].astype(jnp.float32), first[None])
        values = jnp.where(seen, pv_ref[:, here, :].astype(jnp.float32), 0.0)
        key_scr[:, here, :] = keys.astype(jnp.bfloat16)
        val_scr[:, here, :HEAD_DIM] = values.astype(jnp.bfloat16)
        val_scr[:, here, HEAD_DIM:] = seen.astype(jnp.float32).astype(jnp.bfloat16)
    sval_scr[:, :HEAD_DIM] = sv_ref[...]
    sval_scr[:, HEAD_DIM:] = jnp.ones((suf, HEAD_DIM), jnp.bfloat16)

    pkeys = key_scr[...].reshape(blocks * rows, HEAD_DIM)
    pvals = val_scr[...].reshape(blocks * rows, 2 * HEAD_DIM)
    skeys = sk_ref[...]
    svals = sval_scr[...]
    causal = lax.broadcasted_iota(jnp.int32, (suf, suf), 0) >= lax.broadcasted_iota(
        jnp.int32, (suf, suf), 1
    )
    over = (((1,), (1,)), ((), ()))
    for g in range(query_ref.shape[1] // HEAD_DIM):
        cols = slice(g * HEAD_DIM, (g + 1) * HEAD_DIM)
        query = query_ref[:, cols]
        s1 = lax.dot_general(query, pkeys, over, preferred_element_type=jnp.float32)
        s2 = lax.dot_general(query, skeys, over, preferred_element_type=jnp.float32)
        s2 = jnp.where(causal, s2, LOW)
        top = jnp.maximum(
            jnp.max(s1, axis=1, keepdims=True), jnp.max(s2, axis=1, keepdims=True)
        )
        w1 = jnp.exp2((s1 - top) * factor).astype(jnp.bfloat16)
        w2 = jnp.exp2((s2 - top) * factor).astype(jnp.bfloat16)
        sums = jnp.dot(w1, pvals, preferred_element_type=jnp.float32)
        sums = sums + jnp.dot(w2, svals, preferred_element_type=jnp.float32)
        out_ref[:, cols] = (sums[:, :HEAD_DIM] / sums[:, HEAD_DIM:]).astype(out_ref.dtype)


def attend(table, me, queries, suffix_keys, suffix_values, prefix):
    suf, width = queries.shape
    heads = suffix_keys.shape[1] // HEAD_DIM
    blocks = prefix.shape[0] // (2 * heads)
    qwidth = width // heads
    rows = DEPTH * BLK
    return pl.pallas_call(
        attend_kernel,
        out_shape=jax.ShapeDtypeStruct((suf, width), jnp.bfloat16),
        grid_spec=pltpu.PrefetchScalarGridSpec(
            num_scalar_prefetch=2,
            grid=(heads,),
            in_specs=[
                pl.BlockSpec((suf, qwidth), lambda j, *_: (0, j)),
                pl.BlockSpec((suf, HEAD_DIM), lambda j, *_: (0, j)),
                pl.BlockSpec((suf, HEAD_DIM), lambda j, *_: (0, j)),
                pl.BlockSpec((blocks, rows, HEAD_DIM), lambda j, *_: (j, 0, 0)),
                pl.BlockSpec((blocks, rows, HEAD_DIM), lambda j, *_: (heads + j, 0, 0)),
            ],
            out_specs=pl.BlockSpec((suf, qwidth), lambda j, *_: (0, j)),
            scratch_shapes=[
                pltpu.VMEM((blocks, rows, HEAD_DIM), jnp.bfloat16),
                pltpu.VMEM((blocks, rows, 2 * HEAD_DIM), jnp.bfloat16),
                pltpu.VMEM((suf, 2 * HEAD_DIM), jnp.bfloat16),
            ],
        ),
        compiler_params=pltpu.CompilerParams(vmem_limit_bytes=48 << 20),
    )(table, me, queries, suffix_keys, suffix_values, prefix, prefix)


def share_ints(parents, node_len, req_leaf):
    axes = ("req", "head")
    count = lax.axis_size("req") * lax.axis_size("head")
    me = lax.axis_index("req") * lax.axis_size("head") + lax.axis_index("head")
    slots = jnp.arange(count, dtype=jnp.int32) == me
    zero = jnp.zeros((count,), jnp.int32)
    table = jnp.concatenate(
        [jnp.where(slots, x[0], 0) for x in (parents, node_len, req_leaf)] + [zero]
    )
    table = table.reshape(-1, 128)
    for bits in ((0, 1), (5, 6), (7,), (3, 4), (2,)):
        flips = [0]
        for bit in bits:
            flips += [flip | 1 << bit for flip in flips]
        total = table
        for flip in flips[1:]:
            total = total + lax.ppermute(table, axes, [(i, i ^ flip) for i in range(count)])
        table = total
    return table.reshape(-1)


def per_device(
    queries, suffix_keys, suffix_values, node_keys, node_values, parents, node_len, req_leaf
):
    reqs = lax.axis_size("req")
    sent = spread(node_keys[0], node_values[0], lax.axis_size("head"))
    pieces = lax.all_to_all(sent, ("req", "head"), split_axis=0, concat_axis=0, tiled=True)
    table = share_ints(parents, node_len, req_leaf)
    picked = pick(table, pieces, reqs)
    prefix = lax.all_to_all(picked, "req", split_axis=0, concat_axis=0, tiled=True)
    me = lax.axis_index("req").reshape(1)
    out = attend(table, me, queries[0], suffix_keys[0], suffix_values[0], prefix)
    return out[None]


def solution(mesh):
    in_specs = (
        P("req", None, "head"),
        P("req", None, "head"),
        P("req", None, "head"),
        P(("req", "head"), None, None),
        P(("req", "head"), None, None),
        P(("req", "head")),
        P(("req", "head")),
        P("req"),
    )
    out_specs = P("req", None, "head")
    return jax.shard_map(
        per_device, mesh=mesh, in_specs=in_specs, out_specs=out_specs, check_vma=False
    )
```

```python
import functools
import math

import jax
import jax.numpy as jnp
from jax import lax
from jax.experimental import pallas as pl
from jax.experimental.pallas import tpu as pltpu
from jax.sharding import PartitionSpec as P

HEAD_DIM = 128
DEPTH = 4
BLK = 16
LOW = -1e30


CUTS = 4


def spread_kernel(
    me_ref, parent_ref, len_ref, leaf_ref, keys_ref, values_ref, out_ref, table_ref,
    rows_scr, out_scr, in_sems, out_sems,
):
    _, tok, width = rows_scr.shape
    blocks, heads = tok // BLK, width // HEAD_DIM // 2
    part, chunk = tok // CUTS, 2 * blocks
    loads = []
    for kv, ref in enumerate((keys_ref, values_ref)):
        for c in range(CUTS):
            here = pl.ds(c * part, part)
            loads.append(
                pltpu.make_async_copy(ref.at[here], rows_scr.at[kv, here], in_sems.at[kv * CUTS + c])
            )
    for load in loads:
        load.start()

    nodes = table_ref.shape[0] * table_ref.shape[1] // 4
    spot = lax.broadcasted_iota(jnp.int32, table_ref.shape, 0) * table_ref.shape[1]
    spot = spot + lax.broadcasted_iota(jnp.int32, table_ref.shape, 1) - me_ref[0]
    table = jnp.zeros(table_ref.shape, jnp.int32)
    for at, ref in enumerate((parent_ref, len_ref, leaf_ref)):
        table = jnp.where(spot == at * nodes, ref[0], table)
    table_ref[...] = table

    stores = []
    for kv in range(2):
        for c in range(CUTS):
            loads[kv * CUTS + c].wait()
        for j in range(heads):
            first = (kv * heads + j) * chunk
            for b in range(blocks):
                for group in range(2):
                    col = group * heads + j
                    out_scr[first + 2 * b + group] = rows_scr[
                        kv, b * BLK:(b + 1) * BLK, col * HEAD_DIM:(col + 1) * HEAD_DIM
                    ]
            here = pl.ds(first, chunk)
            stores.append(
                pltpu.make_async_copy(
                    out_scr.at[here], out_ref.at[here], out_sems.at[kv * heads + j]
                )
            )
            stores[-1].start()
    for store in stores:
        store.wait()


def spread(me, parents, node_len, req_leaf, keys, values, count):
    tok, width = keys.shape
    pieces = 2 * (tok // BLK) * (width // HEAD_DIM)
    heads = width // HEAD_DIM // 2
    return pl.pallas_call(
        spread_kernel,
        out_shape=(
            jax.ShapeDtypeStruct((pieces, BLK, HEAD_DIM), keys.dtype),
            jax.ShapeDtypeStruct((4 * count // 128, 128), jnp.int32),
        ),
        in_specs=[pl.BlockSpec(memory_space=pltpu.SMEM)] * 4
        + [pl.BlockSpec(memory_space=pl.ANY)] * 2,
        out_specs=(
            pl.BlockSpec(memory_space=pl.ANY),
            pl.BlockSpec(memory_space=pltpu.VMEM),
        ),
        scratch_shapes=[
            pltpu.VMEM((2, tok, width), keys.dtype),
            pltpu.VMEM((pieces, BLK, HEAD_DIM), keys.dtype),
            pltpu.SemaphoreType.DMA((2 * CUTS,)),
            pltpu.SemaphoreType.DMA((2 * heads,)),
        ],
        compiler_params=pltpu.CompilerParams(vmem_limit_bytes=60 << 20),
    )(me, parents, node_len, req_leaf, keys, values)


def pick_kernel(reqs_step, table_ref, pieces_ref, out_ref):
    nodes = pieces_ref.shape[0]
    base = pl.program_id(0) * reqs_step

    def one(r, carry):
        node = table_ref[2 * nodes + 2 * (base + r)]
        for i in range(DEPTH):
            out_ref[r, i * BLK:(i + 1) * BLK, :] = pieces_ref[node]
            if i < DEPTH - 1:
                node = table_ref[node]
        return carry

    lax.fori_loop(0, reqs_step, one, 0, unroll=8)


def pick(table, pieces, reqs):
    steps = 4
    reqs_step = reqs // steps
    return pl.pallas_call(
        functools.partial(pick_kernel, reqs_step),
        out_shape=jax.ShapeDtypeStruct((reqs, DEPTH * BLK, HEAD_DIM), pieces.dtype),
        grid_spec=pltpu.PrefetchScalarGridSpec(
            num_scalar_prefetch=1,
            grid=(steps,),
            in_specs=[pl.BlockSpec(pieces.shape, lambda s, t: (0, 0, 0))],
            out_specs=pl.BlockSpec((reqs_step, DEPTH * BLK, HEAD_DIM), lambda s, t: (s, 0, 0)),
        ),
        compiler_params=pltpu.CompilerParams(vmem_limit_bytes=32 << 20),
    )(table, pieces)


def attend_kernel(
    table_ref, me_ref, query_ref, sk_ref, sv_ref, pk_ref, pv_ref, out_ref,
    key_scr, val_scr, sval_scr,
):
    nodes = table_ref.shape[0] // 4
    blocks = pk_ref.shape[0]
    rows = DEPTH * BLK
    suf = sk_ref.shape[0]
    factor = math.log2(math.e) / math.sqrt(HEAD_DIM)

    node = table_ref[2 * nodes + 2 * me_ref[0]]
    spans = []
    for i in range(DEPTH):
        spans.append(table_ref[nodes + node])
        if i < DEPTH - 1:
            node = table_ref[node]
    tok = lax.broadcasted_iota(jnp.int32, (blocks, BLK, HEAD_DIM), 0) * BLK
    tok = tok + lax.broadcasted_iota(jnp.int32, (blocks, BLK, HEAD_DIM), 1)
    for i in range(DEPTH):
        here = slice(i * BLK, (i + 1) * BLK)
        seen = tok < spans[i]
        first = pk_ref[0, i * BLK:i * BLK + 1, :].astype(jnp.float32)
        keys = jnp.where(seen, pk_ref[:, here, :].astype(jnp.float32), first[None])
        values = jnp.where(seen, pv_ref[:, here, :].astype(jnp.float32), 0.0)
        key_scr[:, here, :] = keys.astype(jnp.bfloat16)
        val_scr[:, here, :HEAD_DIM] = values.astype(jnp.bfloat16)
        val_scr[:, here, HEAD_DIM:] = seen.astype(jnp.float32).astype(jnp.bfloat16)
    sval_scr[:, :HEAD_DIM] = sv_ref[...]
    sval_scr[:, HEAD_DIM:] = jnp.ones((suf, HEAD_DIM), jnp.bfloat16)

    pkeys = key_scr[...].reshape(blocks * rows, HEAD_DIM)
    pvals = val_scr[...].reshape(blocks * rows, 2 * HEAD_DIM)
    skeys = sk_ref[...]
    svals = sval_scr[...]
    causal = lax.broadcasted_iota(jnp.int32, (suf, suf), 0) >= lax.broadcasted_iota(
        jnp.int32, (suf, suf), 1
    )
    over = (((1,), (1,)), ((), ()))
    for g in range(query_ref.shape[1] // HEAD_DIM):
        cols = slice(g * HEAD_DIM, (g + 1) * HEAD_DIM)
        query = query_ref[:, cols]
        s1 = lax.dot_general(query, pkeys, over, preferred_element_type=jnp.float32)
        s2 = lax.dot_general(query, skeys, over, preferred_element_type=jnp.float32)
        s2 = jnp.where(causal, s2, LOW)
        top = jnp.maximum(
            jnp.max(s1, axis=1, keepdims=True), jnp.max(s2, axis=1, keepdims=True)
        )
        w1 = jnp.exp2((s1 - top) * factor).astype(jnp.bfloat16)
        w2 = jnp.exp2((s2 - top) * factor).astype(jnp.bfloat16)
        sums = jnp.dot(w1, pvals, preferred_element_type=jnp.float32)
        sums = sums + jnp.dot(w2, svals, preferred_element_type=jnp.float32)
        out_ref[:, cols] = (sums[:, :HEAD_DIM] / sums[:, HEAD_DIM:]).astype(out_ref.dtype)


def attend(table, me, queries, suffix_keys, suffix_values, prefix):
    suf, width = queries.shape
    heads = suffix_keys.shape[1] // HEAD_DIM
    blocks = prefix.shape[0] // (2 * heads)
    qwidth = width // heads
    rows = DEPTH * BLK
    return pl.pallas_call(
        attend_kernel,
        out_shape=jax.ShapeDtypeStruct((suf, width), jnp.bfloat16),
        grid_spec=pltpu.PrefetchScalarGridSpec(
            num_scalar_prefetch=2,
            grid=(heads,),
            in_specs=[
                pl.BlockSpec((suf, qwidth), lambda j, *_: (0, j)),
                pl.BlockSpec((suf, HEAD_DIM), lambda j, *_: (0, j)),
                pl.BlockSpec((suf, HEAD_DIM), lambda j, *_: (0, j)),
                pl.BlockSpec((blocks, rows, HEAD_DIM), lambda j, *_: (j, 0, 0)),
                pl.BlockSpec((blocks, rows, HEAD_DIM), lambda j, *_: (heads + j, 0, 0)),
            ],
            out_specs=pl.BlockSpec((suf, qwidth), lambda j, *_: (0, j)),
            scratch_shapes=[
                pltpu.VMEM((blocks, rows, HEAD_DIM), jnp.bfloat16),
                pltpu.VMEM((blocks, rows, 2 * HEAD_DIM), jnp.bfloat16),
                pltpu.VMEM((suf, 2 * HEAD_DIM), jnp.bfloat16),
            ],
        ),
        compiler_params=pltpu.CompilerParams(vmem_limit_bytes=48 << 20),
    )(table, me, queries, suffix_keys, suffix_values, prefix, prefix)


def share_ints(table, count):
    for bits in ((0, 1), (5, 6), (7,), (3, 4), (2,)):
        flips = [0]
        for bit in bits:
            flips += [flip | 1 << bit for flip in flips]
        total = table
        for flip in flips[1:]:
            total = total + lax.ppermute(
                table, ("req", "head"), [(i, i ^ flip) for i in range(count)]
            )
        table = total
    return table.reshape(-1)


def per_device(
    queries, suffix_keys, suffix_values, node_keys, node_values, parents, node_len, req_leaf
):
    reqs, groups = lax.axis_size("req"), lax.axis_size("head")
    me = lax.axis_index("req").reshape(1)
    flat = me * groups + lax.axis_index("head")
    sent, table = spread(
        flat, parents, node_len, req_leaf, node_keys[0], node_values[0], reqs * groups
    )
    pieces = lax.all_to_all(sent, ("req", "head"), split_axis=0, concat_axis=0, tiled=True)
    table = share_ints(table, reqs * groups)
    picked = pick(table, pieces, reqs)
    prefix = lax.all_to_all(picked, "req", split_axis=0, concat_axis=0, tiled=True)
    out = attend(table, me, queries[0], suffix_keys[0], suffix_values[0], prefix)
    return out[None]


def solution(mesh):
    in_specs = (
        P("req", None, "head"),
        P("req", None, "head"),
        P("req", None, "head"),
        P(("req", "head"), None, None),
        P(("req", "head"), None, None),
        P(("req", "head")),
        P(("req", "head")),
        P("req"),
    )
    out_specs = P("req", None, "head")
    return jax.shard_map(
        per_device, mesh=mesh, in_specs=in_specs, out_specs=out_specs, check_vma=False
    )
```

```python
import functools
import math

import jax
import jax.numpy as jnp
from jax import lax
from jax.experimental import pallas as pl
from jax.experimental.pallas import tpu as pltpu
from jax.sharding import PartitionSpec as P

HEAD_DIM = 128
DEPTH = 4
BLK = 16
LOW = -1e30


CUTS = 4


def spread_kernel(
    parent_ref, len_ref, leaf_ref, keys_ref, values_ref, out_ref, table_ref,
    rows_scr, out_scr, in_sems, out_sems,
):
    _, tok, width = rows_scr.shape
    blocks, heads = tok // BLK, width // HEAD_DIM // 2
    part, chunk = tok // CUTS, 2 * blocks
    loads = []
    for kv, ref in enumerate((keys_ref, values_ref)):
        for c in range(CUTS):
            here = pl.ds(c * part, part)
            loads.append(
                pltpu.make_async_copy(ref.at[here], rows_scr.at[kv, here], in_sems.at[kv * CUTS + c])
            )
    for load in loads:
        load.start()

    stores = []
    for kv in range(2):
        for c in range(CUTS):
            loads[kv * CUTS + c].wait()
        for j in range(heads):
            first = (kv * heads + j) * chunk
            for b in range(blocks):
                for group in range(2):
                    col = group * heads + j
                    out_scr[first + 2 * b + group] = rows_scr[
                        kv, b * BLK:(b + 1) * BLK, col * HEAD_DIM:(col + 1) * HEAD_DIM
                    ]
            here = pl.ds(first, chunk)
            stores.append(
                pltpu.make_async_copy(
                    out_scr.at[here], out_ref.at[here], out_sems.at[kv * heads + j]
                )
            )
            stores[-1].start()
    me = lax.axis_index("req") * lax.axis_size("head") + lax.axis_index("head")
    nodes = table_ref.shape[0] * table_ref.shape[1] // 4
    spot = lax.broadcasted_iota(jnp.int32, table_ref.shape, 0) * table_ref.shape[1]
    spot = spot + lax.broadcasted_iota(jnp.int32, table_ref.shape, 1) - me
    table = jnp.zeros(table_ref.shape, jnp.int32)
    for i, ref in enumerate((parent_ref, len_ref, leaf_ref)):
        table = jnp.where(spot == i * nodes, ref[...], table)
    table_ref[...] = table

    for store in stores:
        store.wait()


def spread(parents, node_len, req_leaf, keys, values, count):
    tok, width = keys.shape
    pieces = 2 * (tok // BLK) * (width // HEAD_DIM)
    heads = width // HEAD_DIM // 2
    return pl.pallas_call(
        spread_kernel,
        out_shape=(
            jax.ShapeDtypeStruct((pieces, BLK, HEAD_DIM), keys.dtype),
            jax.ShapeDtypeStruct((4 * count // 128, 128), jnp.int32),
        ),
        in_specs=[pl.BlockSpec(memory_space=pltpu.VMEM)] * 3
        + [pl.BlockSpec(memory_space=pl.ANY)] * 2,
        out_specs=(
            pl.BlockSpec(memory_space=pl.ANY),
            pl.BlockSpec(memory_space=pltpu.VMEM),
        ),
        scratch_shapes=[
            pltpu.VMEM((2, tok, width), keys.dtype),
            pltpu.VMEM((pieces, BLK, HEAD_DIM), keys.dtype),
            pltpu.SemaphoreType.DMA((2 * CUTS,)),
            pltpu.SemaphoreType.DMA((2 * heads,)),
        ],
        compiler_params=pltpu.CompilerParams(vmem_limit_bytes=60 << 20),
    )(*(x.reshape(1, 1) for x in (parents, node_len, req_leaf)), keys, values)


def pick_kernel(reqs_step, table_ref, pieces_ref, out_ref):
    nodes = pieces_ref.shape[0]
    base = pl.program_id(0) * reqs_step

    def one(r, carry):
        node = table_ref[2 * nodes + 2 * (base + r)]
        for i in range(DEPTH):
            out_ref[r, i * BLK:(i + 1) * BLK, :] = pieces_ref[node]
            if i < DEPTH - 1:
                node = table_ref[node]
        return carry

    lax.fori_loop(0, reqs_step, one, 0, unroll=8)


def pick(table, pieces, reqs):
    steps = 4
    reqs_step = reqs // steps
    return pl.pallas_call(
        functools.partial(pick_kernel, reqs_step),
        out_shape=jax.ShapeDtypeStruct((reqs, DEPTH * BLK, HEAD_DIM), pieces.dtype),
        grid_spec=pltpu.PrefetchScalarGridSpec(
            num_scalar_prefetch=1,
            grid=(steps,),
            in_specs=[pl.BlockSpec(pieces.shape, lambda s, t: (0, 0, 0))],
            out_specs=pl.BlockSpec((reqs_step, DEPTH * BLK, HEAD_DIM), lambda s, t: (s, 0, 0)),
        ),
        compiler_params=pltpu.CompilerParams(vmem_limit_bytes=32 << 20),
    )(table, pieces)


FACTOR = math.log2(math.e) / math.sqrt(HEAD_DIM)
OVER = (((1,), (1,)), ((), ()))


def attend_kernel(
    table_ref, query_ref, sk_ref, sv_ref, prefix_ref, out_ref,
    key_scr, val_scr, out_scr, sems,
):
    nodes = table_ref.shape[0] // 4
    suf = sk_ref.shape[0]
    heads = sk_ref.shape[1] // HEAD_DIM
    blocks, rows = prefix_ref.shape[0] // (2 * heads), prefix_ref.shape[1]
    cached = blocks * rows
    group = query_ref.shape[1] // HEAD_DIM // heads

    node = table_ref[2 * nodes + 2 * lax.axis_index("req")]
    spans = []
    for i in range(DEPTH):
        spans.append(table_ref[nodes + node])
        if i < DEPTH - 1:
            node = table_ref[node]
    shape = (blocks, BLK, HEAD_DIM)
    tok = lax.broadcasted_iota(jnp.int32, shape, 0) * BLK
    tok = tok + lax.broadcasted_iota(jnp.int32, shape, 1)
    seen = [tok < span for span in spans]
    row = lax.broadcasted_iota(jnp.int32, (suf, suf), 0)
    causal = row >= lax.broadcasted_iota(jnp.int32, (suf, suf), 1)

    shown = jnp.stack([x.astype(jnp.float32).astype(jnp.bfloat16) for x in seen], axis=1)
    shown = shown.reshape(cached, HEAD_DIM)
    for slot in range(val_scr.shape[0]):
        val_scr[slot, :cached, HEAD_DIM:] = shown
        val_scr[slot, cached:, HEAD_DIM:] = jnp.ones((suf, HEAD_DIM), val_scr.dtype)

    def prepare(j):
        slot = j % val_scr.shape[0]
        keys, values = [], []
        for i in range(DEPTH):
            here = slice(i * BLK, (i + 1) * BLK)
            key = prefix_ref[j * blocks:(j + 1) * blocks, here, :].astype(jnp.float32)
            keys.append(jnp.where(seen[i], key, key[:1, :1]).astype(jnp.bfloat16))
            value = prefix_ref[(heads + j) * blocks:(heads + j + 1) * blocks, here, :]
            values.append(jnp.where(seen[i], value.astype(jnp.float32), 0.0).astype(jnp.bfloat16))
        own = slice(j * HEAD_DIM, (j + 1) * HEAD_DIM)
        key_scr[slot, :cached] = jnp.stack(keys, axis=1).reshape(cached, HEAD_DIM)
        val_scr[slot, :cached, :HEAD_DIM] = jnp.stack(values, axis=1).reshape(cached, HEAD_DIM)
        key_scr[slot, cached:] = sk_ref[:, own]
        val_scr[slot, cached:, :HEAD_DIM] = sv_ref[:, own]

    def scores_of(item):
        j = item // group
        if item % group == 0:
            prepare(j)
        query = query_ref[:, item * HEAD_DIM:(item + 1) * HEAD_DIM]
        return lax.dot_general(
            query, key_scr[j % key_scr.shape[0]], OVER, preferred_element_type=jnp.float32
        )

    stores = []
    for item in range(heads * group):
        j, g = divmod(item, group)
        scores = scores_of(item)
        old, new = scores[:, :cached], jnp.where(causal, scores[:, cached:], LOW)
        top = jnp.maximum(
            jnp.max(old, axis=1, keepdims=True), jnp.max(new, axis=1, keepdims=True)
        )
        weights = jnp.concatenate(
            [jnp.exp2((x - top) * FACTOR).astype(jnp.bfloat16) for x in (old, new)], axis=1
        )
        sums = jnp.dot(
            weights, val_scr[j % val_scr.shape[0]], preferred_element_type=jnp.float32
        )
        attended = sums[:, :HEAD_DIM] / sums[:, HEAD_DIM:]
        out_scr[j, :, g * HEAD_DIM:(g + 1) * HEAD_DIM] = attended.astype(out_scr.dtype)
        if g == group - 1:
            at = pl.ds(j * group * HEAD_DIM, group * HEAD_DIM)
            stores.append(
                pltpu.make_async_copy(out_scr.at[j], out_ref.at[:, at], sems.at[j])
            )
            stores[-1].start()
    for store in stores:
        store.wait()


def attend(table, queries, suffix_keys, suffix_values, prefix):
    suf, width = queries.shape
    heads = suffix_keys.shape[1] // HEAD_DIM
    total = prefix.shape[0] // (2 * heads) * prefix.shape[1] + suf
    return pl.pallas_call(
        attend_kernel,
        out_shape=jax.ShapeDtypeStruct((suf, width), jnp.bfloat16),
        in_specs=[pl.BlockSpec(memory_space=pltpu.SMEM)]
        + [pl.BlockSpec(memory_space=pltpu.VMEM)] * 4,
        out_specs=pl.BlockSpec(memory_space=pl.ANY),
        scratch_shapes=[
            pltpu.VMEM((2, total, HEAD_DIM), jnp.bfloat16),
            pltpu.VMEM((2, total, 2 * HEAD_DIM), jnp.bfloat16),
            pltpu.VMEM((heads, suf, width // heads), jnp.bfloat16),
            pltpu.SemaphoreType.DMA((heads,)),
        ],
        compiler_params=pltpu.CompilerParams(vmem_limit_bytes=40 << 20),
    )(table, queries, suffix_keys, suffix_values, prefix)


def share_ints(table, count):
    for bits in ((0, 1), (5, 6), (7,), (3, 4), (2,)):
        flips = [0]
        for bit in bits:
            flips += [flip | 1 << bit for flip in flips]
        total = table
        for flip in flips[1:]:
            total = total + lax.ppermute(
                table, ("req", "head"), [(i, i ^ flip) for i in range(count)]
            )
        table = total
    return table.reshape(-1)


def per_device(
    queries, suffix_keys, suffix_values, node_keys, node_values, parents, node_len, req_leaf
):
    reqs, groups = lax.axis_size("req"), lax.axis_size("head")
    sent, table = spread(
        parents, node_len, req_leaf, node_keys[0], node_values[0], reqs * groups
    )
    pieces = lax.all_to_all(sent, ("req", "head"), split_axis=0, concat_axis=0, tiled=True)
    table = share_ints(table, reqs * groups)
    picked = pick(table, pieces, reqs)
    prefix = lax.all_to_all(picked, "req", split_axis=0, concat_axis=0, tiled=True)
    out = attend(table, queries[0], suffix_keys[0], suffix_values[0], prefix)
    return out[None]


def solution(mesh):
    in_specs = (
        P("req", None, "head"),
        P("req", None, "head"),
        P("req", None, "head"),
        P(("req", "head"), None, None),
        P(("req", "head"), None, None),
        P(("req", "head")),
        P(("req", "head")),
        P("req"),
    )
    out_specs = P("req", None, "head")
    return jax.shard_map(
        per_device, mesh=mesh, in_specs=in_specs, out_specs=out_specs, check_vma=False
    )
```

```python
import functools
import math

import jax
import jax.numpy as jnp
from jax import lax
from jax.experimental import pallas as pl
from jax.experimental.pallas import tpu as pltpu
from jax.sharding import PartitionSpec as P

HEAD_DIM = 128
DEPTH = 4
BLK = 16
LOW = -1e30


CUTS = 4


def spread_kernel(
    parent_ref, len_ref, leaf_ref, keys_ref, values_ref, out_ref, table_ref,
    rows_scr, out_scr, table_scr, in_sems, out_sems, table_sem,
):
    _, tok, width = rows_scr.shape
    blocks, heads = tok // BLK, width // HEAD_DIM // 2
    part, chunk = tok // CUTS, 2 * blocks
    loads = []
    for kv, ref in enumerate((keys_ref, values_ref)):
        for c in range(CUTS):
            here = pl.ds(c * part, part)
            loads.append(
                pltpu.make_async_copy(ref.at[here], rows_scr.at[kv, here], in_sems.at[kv * CUTS + c])
            )
    for load in loads:
        load.start()

    me = lax.axis_index("req") * lax.axis_size("head") + lax.axis_index("head")
    nodes = table_scr.shape[0] * table_scr.shape[1] // 4
    spot = lax.broadcasted_iota(jnp.int32, table_scr.shape, 0) * table_scr.shape[1]
    spot = spot + lax.broadcasted_iota(jnp.int32, table_scr.shape, 1) - me
    table = jnp.zeros(table_scr.shape, jnp.int32)
    for i, ref in enumerate((parent_ref, len_ref, leaf_ref)):
        table = jnp.where(spot == i * nodes, ref[0], table)
    table_scr[...] = table
    stores = [pltpu.make_async_copy(table_scr, table_ref, table_sem)]
    stores[0].start()

    for kv in range(2):
        for c in range(CUTS):
            loads[kv * CUTS + c].wait()
        for j in range(heads):
            first = (kv * heads + j) * chunk
            for b in range(blocks):
                for group in range(2):
                    col = group * heads + j
                    out_scr[first + 2 * b + group] = rows_scr[
                        kv, b * BLK:(b + 1) * BLK, col * HEAD_DIM:(col + 1) * HEAD_DIM
                    ]
            here = pl.ds(first, chunk)
            stores.append(
                pltpu.make_async_copy(
                    out_scr.at[here], out_ref.at[here], out_sems.at[kv * heads + j]
                )
            )
            stores[-1].start()
    for store in stores:
        store.wait()


def spread(parents, node_len, req_leaf, keys, values, count):
    tok, width = keys.shape
    pieces = 2 * (tok // BLK) * (width // HEAD_DIM)
    heads = width // HEAD_DIM // 2
    return pl.pallas_call(
        spread_kernel,
        out_shape=(
            jax.ShapeDtypeStruct((pieces, BLK, HEAD_DIM), keys.dtype),
            jax.ShapeDtypeStruct((4 * count // 128, 128), jnp.int32),
        ),
        in_specs=[pl.BlockSpec(memory_space=pltpu.SMEM)] * 3
        + [pl.BlockSpec(memory_space=pl.ANY)] * 2,
        out_specs=(pl.BlockSpec(memory_space=pl.ANY),) * 2,
        scratch_shapes=[
            pltpu.VMEM((2, tok, width), keys.dtype),
            pltpu.VMEM((pieces, BLK, HEAD_DIM), keys.dtype),
            pltpu.VMEM((4 * count // 128, 128), jnp.int32),
            pltpu.SemaphoreType.DMA((2 * CUTS,)),
            pltpu.SemaphoreType.DMA((2 * heads,)),
            pltpu.SemaphoreType.DMA,
        ],
        compiler_params=pltpu.CompilerParams(vmem_limit_bytes=60 << 20),
    )(parents, node_len, req_leaf, keys, values)


def pick_kernel(table_ref, pieces_ref, out_ref):
    nodes = pieces_ref.shape[0]

    def one(r, carry):
        node = table_ref[2 * nodes + 2 * r]
        for i in range(DEPTH):
            out_ref[r, i * BLK:(i + 1) * BLK, :] = pieces_ref[node]
            if i < DEPTH - 1:
                node = table_ref[node]
        return carry

    lax.fori_loop(0, out_ref.shape[0], one, 0, unroll=8)


def pick(table, pieces, reqs):
    return pl.pallas_call(
        pick_kernel,
        out_shape=jax.ShapeDtypeStruct((reqs, DEPTH * BLK, HEAD_DIM), pieces.dtype),
        in_specs=[
            pl.BlockSpec(memory_space=pltpu.SMEM),
            pl.BlockSpec(memory_space=pltpu.VMEM),
        ],
        out_specs=pl.BlockSpec(memory_space=pltpu.VMEM),
        compiler_params=pltpu.CompilerParams(vmem_limit_bytes=32 << 20),
    )(table, pieces)


FACTOR = math.log2(math.e) / math.sqrt(HEAD_DIM)
OVER = (((1,), (1,)), ((), ()))


def attend_kernel(
    table_ref, query_ref, sk_ref, sv_ref, prefix_ref, out_ref,
    key_scr, val_scr, out_scr, sems,
):
    nodes = table_ref.shape[0] // 4
    suf = sk_ref.shape[0]
    heads = sk_ref.shape[1] // HEAD_DIM
    blocks, rows = prefix_ref.shape[0] // (2 * heads), prefix_ref.shape[1]
    cached = blocks * rows
    group = query_ref.shape[1] // HEAD_DIM // heads

    node = table_ref[2 * nodes + 2 * lax.axis_index("req")]
    spans = []
    for i in range(DEPTH):
        spans.append(table_ref[nodes + node])
        if i < DEPTH - 1:
            node = table_ref[node]
    shape = (blocks, BLK, HEAD_DIM)
    tok = lax.broadcasted_iota(jnp.int32, shape, 0) * BLK
    tok = tok + lax.broadcasted_iota(jnp.int32, shape, 1)
    seen = [tok < span for span in spans]
    row = lax.broadcasted_iota(jnp.int32, (suf, suf), 0)
    causal = row >= lax.broadcasted_iota(jnp.int32, (suf, suf), 1)

    shown = jnp.stack([x.astype(jnp.float32).astype(jnp.bfloat16) for x in seen], axis=1)
    shown = shown.reshape(cached, HEAD_DIM)
    for slot in range(val_scr.shape[0]):
        val_scr[slot, :cached, HEAD_DIM:] = shown
        val_scr[slot, cached:, HEAD_DIM:] = jnp.ones((suf, HEAD_DIM), val_scr.dtype)

    def prepare(j):
        slot = j % val_scr.shape[0]
        keys, values = [], []
        for i in range(DEPTH):
            here = slice(i * BLK, (i + 1) * BLK)
            key = prefix_ref[j * blocks:(j + 1) * blocks, here, :].astype(jnp.float32)
            keys.append(jnp.where(seen[i], key, key[:1, :1]).astype(jnp.bfloat16))
            value = prefix_ref[(heads + j) * blocks:(heads + j + 1) * blocks, here, :]
            values.append(jnp.where(seen[i], value.astype(jnp.float32), 0.0).astype(jnp.bfloat16))
        own = slice(j * HEAD_DIM, (j + 1) * HEAD_DIM)
        key_scr[slot, :cached] = jnp.stack(keys, axis=1).reshape(cached, HEAD_DIM)
        val_scr[slot, :cached, :HEAD_DIM] = jnp.stack(values, axis=1).reshape(cached, HEAD_DIM)
        key_scr[slot, cached:] = sk_ref[:, own]
        val_scr[slot, cached:, :HEAD_DIM] = sv_ref[:, own]

    def scores_of(item):
        j = item // group
        if item % group == 0:
            prepare(j)
        query = query_ref[:, item * HEAD_DIM:(item + 1) * HEAD_DIM]
        return lax.dot_general(
            query, key_scr[j % key_scr.shape[0]], OVER, preferred_element_type=jnp.float32
        )

    stores = []
    for item in range(heads * group):
        j, g = divmod(item, group)
        scores = scores_of(item)
        old, new = scores[:, :cached], jnp.where(causal, scores[:, cached:], LOW)
        top = jnp.maximum(
            jnp.max(old, axis=1, keepdims=True), jnp.max(new, axis=1, keepdims=True)
        )
        weights = jnp.concatenate(
            [jnp.exp2((x - top) * FACTOR).astype(jnp.bfloat16) for x in (old, new)], axis=1
        )
        sums = jnp.dot(
            weights, val_scr[j % val_scr.shape[0]], preferred_element_type=jnp.float32
        )
        attended = sums[:, :HEAD_DIM] / sums[:, HEAD_DIM:]
        out_scr[j, :, g * HEAD_DIM:(g + 1) * HEAD_DIM] = attended.astype(out_scr.dtype)
        if g == group - 1:
            at = pl.ds(j * group * HEAD_DIM, group * HEAD_DIM)
            stores.append(
                pltpu.make_async_copy(out_scr.at[j], out_ref.at[:, at], sems.at[j])
            )
            stores[-1].start()
    for store in stores:
        store.wait()


def attend(table, queries, suffix_keys, suffix_values, prefix):
    suf, width = queries.shape
    heads = suffix_keys.shape[1] // HEAD_DIM
    total = prefix.shape[0] // (2 * heads) * prefix.shape[1] + suf
    return pl.pallas_call(
        attend_kernel,
        out_shape=jax.ShapeDtypeStruct((suf, width), jnp.bfloat16),
        in_specs=[pl.BlockSpec(memory_space=pltpu.SMEM)]
        + [pl.BlockSpec(memory_space=pltpu.VMEM)] * 4,
        out_specs=pl.BlockSpec(memory_space=pl.ANY),
        scratch_shapes=[
            pltpu.VMEM((2, total, HEAD_DIM), jnp.bfloat16),
            pltpu.VMEM((2, total, 2 * HEAD_DIM), jnp.bfloat16),
            pltpu.VMEM((heads, suf, width // heads), jnp.bfloat16),
            pltpu.SemaphoreType.DMA((heads,)),
        ],
        compiler_params=pltpu.CompilerParams(vmem_limit_bytes=40 << 20),
    )(table, queries, suffix_keys, suffix_values, prefix)


def share_ints(table, count):
    for bits in ((0, 1), (5, 6), (7,), (3, 4), (2,)):
        flips = [0]
        for bit in bits:
            flips += [flip | 1 << bit for flip in flips]
        total = table
        for flip in flips[1:]:
            total = total + lax.ppermute(
                table, ("req", "head"), [(i, i ^ flip) for i in range(count)]
            )
        table = total
    return table.reshape(-1)


def per_device(
    queries, suffix_keys, suffix_values, node_keys, node_values, parents, node_len, req_leaf
):
    reqs, groups = lax.axis_size("req"), lax.axis_size("head")
    sent, table = spread(
        parents, node_len, req_leaf, node_keys[0], node_values[0], reqs * groups
    )
    pieces = lax.all_to_all(sent, ("req", "head"), split_axis=0, concat_axis=0, tiled=True)
    table = share_ints(table, reqs * groups)
    picked = pick(table, pieces, reqs)
    prefix = lax.all_to_all(picked, "req", split_axis=0, concat_axis=0, tiled=True)
    out = attend(table, queries[0], suffix_keys[0], suffix_values[0], prefix)
    return out[None]


def solution(mesh):
    in_specs = (
        P("req", None, "head"),
        P("req", None, "head"),
        P("req", None, "head"),
        P(("req", "head"), None, None),
        P(("req", "head"), None, None),
        P(("req", "head")),
        P(("req", "head")),
        P("req"),
    )
    out_specs = P("req", None, "head")
    return jax.shard_map(
        per_device, mesh=mesh, in_specs=in_specs, out_specs=out_specs, check_vma=False
    )
```
